128 devices in a mesh: col: 4 (over x_hi, core), row: 32 (over z, y, x_lo).
Axes of the slice: x: 4 (x_hi: 2, x_lo: 2; x = x_hi * 2 + x_lo), y: 4, z: 4, core: 2. Of those that a mesh axis runs over, the one named last changes fastest.
Arguments:
- amplitudes: bfloat16 [2, 32, 1536, 1536], P(None, 'row', None, 'col'), may hold values from -6 to 6
- coupling: bfloat16 [2, 1536, 4, 1536], P(None, 'row', None, 'col'), may hold values from -0.109375 to 0.109375
Outputs:
- cycle_term: bfloat16 [32, 1536, 4, 1536], P(None, 'row', None, 'col')
The draws below stay inside these ranges and needn't reach their ends.
All inputs are finite; a program needn't handle non-finite values.
Results may differ from the reference program's by a relative error of at most 0.001.
Values may be sent and summed in bfloat16 or wider, within the bound.
No kernel may reach another device: no remote copies, remote signals or barrier semaphores. Data moves between devices by JAX's collectives and lax.ppermute only.
A program may use at most 128 MiB of HBM per device.

```python
import jax
import jax.numpy as jnp
from jax import lax

V = 1536
NI = 2
NK = 4
NJ = 32


def shard_levels(stream_key, dims, split, low, top_value):
    loudness = 1.0
    for dim, parts in split:
        steps = jax.random.uniform(jax.random.fold_in(jax.random.fold_in(stream_key, 6), dim), (parts,), jnp.float32, low / len(split), top_value / len(split))
        loudness = loudness * jnp.repeat(jnp.exp(steps), dims[dim] // parts).reshape((-1,) + (1,) * (len(dims) - 1 - dim))
    return loudness


def scatter_about(stream_key, dims, spread, reach, shards=(), held_as=jnp.bfloat16):
    entries = spread * jax.random.normal(stream_key, dims, jnp.float32)
    if shards:
        entries = entries * shard_levels(stream_key, dims, shards, -0.22, 0.18)
    return jnp.clip(entries, -reach, reach).astype(held_as)


def setup_inputs(seed: int = 0) -> dict:
    seeds = jax.random.split(jax.random.key(seed), 3)
    return {
        "amplitudes": scatter_about(seeds[0], (NI, NJ, V, V), 1.0, 6.0, ((1, 32), (3, 4))),
        "coupling": scatter_about(seeds[1], (NI, V, NK, V), (NI * V) ** -0.5, 0.109375, ((1, 32), (3, 4))),
    }


def reference(amplitudes, coupling):
    matrix = coupling.reshape(NI * V, NK * V)

    def one_pair(block):
        rows = jnp.transpose(block, (1, 0, 2)).reshape(V, NI * V)
        result = jnp.dot(rows, matrix, preferred_element_type=jnp.float32)
        return result.astype(jnp.bfloat16).reshape(V, NK, V)

    return lax.map(one_pair, jnp.transpose(amplitudes, (1, 0, 2, 3)))
```

```python
import jax
import jax.numpy as jnp
from jax import lax
from jax.sharding import Mesh, PartitionSpec as P

FINE = ("xh", "core", "z", "y", "xl")
ROW = ("z", "y", "xl")
SWAP = [(0, 1), (1, 0)]


def on_device(amplitudes, coupling):
    ni, _, v, qa = amplitudes.shape
    rows = lax.axis_size(ROW)
    nb = v // rows
    na, nk, qc = coupling.shape[1:]
    xh, core = lax.axis_index("xh"), lax.axis_index("core")

    mine = jnp.transpose(coupling, (2, 0, 1, 3))
    other = lax.ppermute(mine, "xl", SWAP)
    first = lax.axis_index("xl") == 0
    pair = jnp.concatenate([jnp.where(first, mine, other), jnp.where(first, other, mine)], axis=2)
    whole = lax.all_gather(pair[None], ("z", "y"), axis=0, tiled=True)
    whole = whole.reshape((4, 4) + pair.shape)

    total = None
    own, far = [], []
    for i in range(ni):
        chunks = amplitudes[i, 0].reshape(rows, nb, qa)
        got = lax.all_to_all(chunks, ROW, split_axis=0, concat_axis=0, tiled=True)
        away = lax.ppermute(got, "xh", SWAP)
        own.append((got, lax.ppermute(got, "core", SWAP)))
        far.append((away, lax.ppermute(away, "core", SWAP)))
    for half, there in ((own, xh), (far, 1 - xh)):
        for i in range(ni):
            for block, c in zip(half[i], (core, 1 - core)):
                matrix = lax.dynamic_index_in_dim(whole, 2 * there + c, 0, keepdims=False)[:, :, i]
                matrix = jnp.transpose(matrix, (0, 2, 1, 3)).reshape(qa, nk, qc)
                term = jnp.einsum("jba,akc->jbkc", block, matrix, preferred_element_type=jnp.float32)
                total = term if total is None else total + term
    return total.astype(jnp.bfloat16)


def solution(mesh):
    fine = Mesh(mesh.devices.reshape(2, 2, 4, 4, 2), FINE)
    placed = P(None, ROW, None, ("xh", "core"))
    return jax.shard_map(
        on_device, mesh=fine, in_specs=(placed, placed), out_specs=placed, check_vma=False
    )
```

```python
import jax
import jax.numpy as jnp
from jax import lax
from jax.experimental import pallas as pl
from jax.experimental.pallas import tpu as pltpu
from jax.sharding import Mesh, PartitionSpec as P

FINE = ("xh", "core", "z", "y", "xl")
ROW = ("z", "y", "xl")
SWAP = [(0, 1), (1, 0)]
TILE = 192


def contract_kernel(place, *refs):
    blocks, (w, out, lhs, mat, total, staged, lsem, wsem, osem) = refs[:8], refs[8:]
    rows, qa = blocks[0].shape
    tiles = rows // TILE
    nk, qc = out.shape[1:]
    xh, core = place[0], place[1]
    steps = [(i, far) for far in (0, 1) for i in (0, 1)]

    def copies(s):
        i, far = steps[s]
        slot = s % 2
        half = 1 - xh if far else xh
        mine, other = blocks[4 * i + 2 * far], blocks[4 * i + 2 * far + 1]
        first = pl.multiple_of(core * qa, 128)
        second = pl.multiple_of((1 - core) * qa, 128)
        return (
            pltpu.make_async_copy(mine, lhs.at[slot, :, pl.ds(first, qa)], lsem.at[slot, 0]),
            pltpu.make_async_copy(other, lhs.at[slot, :, pl.ds(second, qa)], lsem.at[slot, 1]),
            pltpu.make_async_copy(w.at[pl.ds(2 * half, 2), :, i], mat.at[slot], wsem.at[slot]),
        )

    def store(m):
        return pltpu.make_async_copy(
            staged.at[pl.ds(m * TILE, TILE)], out.at[pl.ds(m * TILE, TILE)], osem.at[m]
        )

    for c in copies(0):
        c.start()
    for s in range(len(steps)):
        if s + 1 < len(steps):
            for c in copies(s + 1):
                c.start()
        for c in copies(s):
            c.wait()
        slot = s % 2

        def tile(m, carry, s=s, slot=slot):
            at = pl.ds(pl.multiple_of(m * TILE, TILE), TILE)
            matrix = mat[slot].reshape(2 * qa, nk * qc)
            term = jnp.dot(lhs[slot, at, :], matrix, preferred_element_type=jnp.float32)
            if s:
                term = term + total[at, :]
            if s + 1 < len(steps):
                total[at, :] = term
            else:
                for k in range(nk):
                    staged[at, k, :] = term[:, k * qc : (k + 1) * qc].astype(staged.dtype)
                store(m).start()
            return carry

        lax.fori_loop(0, tiles, tile, 0)
    lax.fori_loop(0, tiles, lambda m, c: (store(m).wait(), c)[1], 0)


def contract(place, blocks, w, nk, qc):
    rows, qa = blocks[0].shape
    tiles = rows // TILE
    any_space = pl.BlockSpec(memory_space=pl.ANY)
    return pl.pallas_call(
        contract_kernel,
        out_shape=jax.ShapeDtypeStruct((rows, nk, qc), jnp.bfloat16),
        in_specs=[pl.BlockSpec(memory_space=pltpu.SMEM)] + [any_space] * 9,
        out_specs=any_space,
        scratch_shapes=[
            pltpu.VMEM((2, rows, 2 * qa), jnp.bfloat16),
            pltpu.VMEM((2, 2) + w.shape[1:2] + w.shape[3:], jnp.bfloat16),
            pltpu.VMEM((rows, nk * qc), jnp.float32),
            pltpu.VMEM((rows, nk, qc), jnp.bfloat16),
            pltpu.SemaphoreType.DMA((2, 2)),
            pltpu.SemaphoreType.DMA((2,)),
            pltpu.SemaphoreType.DMA((tiles,)),
        ],
        compiler_params=pltpu.CompilerParams(vmem_limit_bytes=48 << 20),
        cost_estimate=pl.CostEstimate(
            flops=2 * rows * 8 * qa * nk * qc, bytes_accessed=24 << 20, transcendentals=0
        ),
        name="contract",
    )(place, *blocks, w)


def on_device(amplitudes, coupling):
    ni, _, v, qa = amplitudes.shape
    rows = lax.axis_size(ROW)
    nb = v // rows
    na, nk, qc = coupling.shape[1:]

    mine = coupling.reshape(ni, na, nk * qc)
    other = lax.ppermute(mine, "xl", SWAP)
    first = lax.axis_index("xl") == 0
    pair = jnp.concatenate([jnp.where(first, mine, other), jnp.where(first, other, mine)], axis=1)
    whole = lax.all_gather(pair[None], ("z", "y"), axis=0, tiled=True)
    whole = whole.reshape((4, 4) + pair.shape)

    blocks = []
    for i in range(ni):
        chunks = amplitudes[i, 0].reshape(rows, nb, qa)
        got = lax.all_to_all(chunks, ROW, split_axis=0, concat_axis=0, tiled=True)
        away = lax.ppermute(got, "xh", SWAP)
        blocks += [got, lax.ppermute(got, "core", SWAP), away, lax.ppermute(away, "core", SWAP)]
    blocks = [b.reshape(rows * nb, qa) for b in blocks]
    place = jnp.stack([lax.axis_index("xh"), lax.axis_index("core")]).astype(jnp.int32)
    return contract(place, blocks, whole, nk, qc).reshape(rows, nb, nk, qc)


def solution(mesh):
    fine = Mesh(mesh.devices.reshape(2, 2, 4, 4, 2), FINE)
    placed = P(None, ROW, None, ("xh", "core"))
    return jax.shard_map(
        on_device, mesh=fine, in_specs=(placed, placed), out_specs=placed, check_vma=False
    )
```

```python
import jax
import jax.numpy as jnp
from jax import lax
from jax.experimental import pallas as pl
from jax.experimental.pallas import tpu as pltpu
from jax.sharding import Mesh, PartitionSpec as P

FINE = ("xh", "core", "z", "y", "xl")
ROW = ("z", "y", "xl")
SWAP = [(0, 1), (1, 0)]
UP = [(n, (n + 1) % 4) for n in range(4)]
DOWN = [(n, (n - 1) % 4) for n in range(4)]
ACROSS = [(n, (n + 2) % 4) for n in range(4)]
TILE = 384
OFFSETS = (0, 3, 1, 2)


def contract_kernel(place, *refs):
    blocks, gathered, (out, lhs, mat, total, staged, lsem, wsem, osem) = refs[:8], refs[8:18], refs[18:]
    rows, qa = blocks[0].shape
    nk, qc = out.shape[1:]
    xh, core, z0, y0 = place[0], place[1], place[2], place[3]
    steps = [(i, far) for far in (0, 1) for i in (0, 1)]

    def planes(i):
        own, low, high, first, last = gathered[5 * i : 5 * i + 5]
        for offset, ref in zip(OFFSETS, (own, low, high)):
            yield offset, [(n, ref, n) for n in range(4)]
        yield OFFSETS[3], [(n, (first, last)[n // 2], n % 2) for n in range(4)]

    def start_matrix(s):
        i, far = steps[s]
        slot = s % 2
        half = 1 - xh if far else xh
        for outer, inner in planes(i):
            for n, ref, index in inner:
                if i == 0:
                    z, y = lax.rem(z0 + outer, 4), lax.rem(y0 + OFFSETS[n], 4)
                else:
                    z, y = lax.rem(z0 + OFFSETS[n], 4), lax.rem(y0 + outer, 4)

                @pl.when(z // 2 == half)
                def _(z=z, y=y, ref=ref, index=index):
                    pltpu.make_async_copy(
                        ref.at[index], mat.at[slot, lax.rem(z, 2), y], wsem.at[slot]
                    ).start()

    def wait_matrix(s):
        pltpu.make_async_copy(mat.at[s % 2], mat.at[s % 2], wsem.at[s % 2]).wait()

    def lhs_copies(s):
        i, far = steps[s]
        slot = s % 2
        mine, other = blocks[4 * i + 2 * far], blocks[4 * i + 2 * far + 1]
        first = pl.multiple_of(core * qa, 128)
        second = pl.multiple_of((1 - core) * qa, 128)
        return (
            pltpu.make_async_copy(mine, lhs.at[slot, :, pl.ds(first, qa)], lsem.at[slot, 0]),
            pltpu.make_async_copy(other, lhs.at[slot, :, pl.ds(second, qa)], lsem.at[slot, 1]),
        )

    def start(s):
        start_matrix(s)
        for c in lhs_copies(s):
            c.start()

    start(0)
    stores = []
    for s in range(len(steps)):
        if s + 1 < len(steps):
            start(s + 1)
        wait_matrix(s)
        for c in lhs_copies(s):
            c.wait()
        slot = s % 2
        matrix = mat[slot].reshape(2 * qa, nk * qc)
        for m in range(rows // TILE):
            at = pl.ds(m * TILE, TILE)
            term = jnp.dot(lhs[slot, at, :], matrix, preferred_element_type=jnp.float32)
            if s:
                term = term + total[at, :]
            if s + 1 < len(steps):
                total[at, :] = term
            else:
                staged[at] = term.astype(staged.dtype).reshape(TILE, nk, qc)
                stores.append(pltpu.make_async_copy(staged.at[at], out.at[at], osem.at[m]))
                stores[-1].start()
    for c in stores:
        c.wait()


def contract(place, blocks, gathered, nk, qc):
    rows, qa = blocks[0].shape
    any_space = pl.BlockSpec(memory_space=pl.ANY)
    return pl.pallas_call(
        contract_kernel,
        out_shape=jax.ShapeDtypeStruct((rows, nk, qc), jnp.bfloat16),
        in_specs=[pl.BlockSpec(memory_space=pltpu.SMEM)] + [any_space] * 18,
        out_specs=any_space,
        scratch_shapes=[
            pltpu.VMEM((2, rows, 2 * qa), jnp.bfloat16),
            pltpu.VMEM((2, 2, 4) + gathered[0].shape[1:], jnp.bfloat16),
            pltpu.VMEM((rows, nk * qc), jnp.float32),
            pltpu.VMEM((rows, nk, qc), jnp.bfloat16),
            pltpu.SemaphoreType.DMA((2, 2)),
            pltpu.SemaphoreType.DMA((2,)),
            pltpu.SemaphoreType.DMA((rows // TILE,)),
        ],
        compiler_params=pltpu.CompilerParams(vmem_limit_bytes=48 << 20),
        cost_estimate=pl.CostEstimate(
            flops=2 * rows * 8 * qa * nk * qc, bytes_accessed=24 << 20, transcendentals=0
        ),
        name="contract",
    )(place, *blocks, *gathered)


def inner_ring(block, axis):
    moved = [lax.ppermute(block, axis, way) for way in (UP, DOWN, ACROSS)]
    return jnp.concatenate([block] + moved, axis=0)


def outer_ring(held, axis):
    return lax.ppermute(held, axis, UP), lax.ppermute(held, axis, DOWN)


def opposite(low, high, axis):
    return lax.ppermute(low[:2], axis, UP), lax.ppermute(high[2:], axis, DOWN)


def on_device(amplitudes, coupling):
    ni, _, v, qa = amplitudes.shape
    rows = lax.axis_size(ROW)
    nb = v // rows
    na, nk, qc = coupling.shape[1:]
    tie = lax.optimization_barrier

    def to_owners(i):
        chunks = amplitudes[i, 0].reshape(rows, nb, qa)
        return lax.all_to_all(chunks, ROW, split_axis=0, concat_axis=0, tiled=True)

    def cross(block):
        return lax.ppermute(block, "xh", SWAP)

    def beside(block):
        return lax.ppermute(block, "core", SWAP)

    mine = coupling.reshape(ni, na, nk * qc)
    other = lax.ppermute(mine, "xl", SWAP)
    lower = lax.axis_index("xl") == 0
    pair = jnp.concatenate([jnp.where(lower, mine, other), jnp.where(lower, other, mine)], axis=1)
    own0 = to_owners(0)
    w0 = inner_ring(pair[0][None], "y")
    w1 = inner_ring(pair[1][None], "z")
    own0, w0, w1, amplitudes = tie((own0, w0, w1, amplitudes))

    far0 = cross(own0)
    own1 = to_owners(1)
    low0, high0 = outer_ring(w0, "z")
    low1, high1 = outer_ring(w1, "y")
    own1, far0 = tie((own1, far0))

    far1 = cross(own1)
    opp0 = opposite(low0, high0, "z")
    opp1 = opposite(low1, high1, "y")
    opp0, opp1, own0, own1, far0 = tie((opp0, opp1, own0, own1, far0))

    own0c, own1c, far0c = beside(own0), beside(own1), beside(far0)
    far1, own0c, own1c, far0c = tie((far1, own0c, own1c, far0c))
    far1c = beside(far1)

    blocks = (own0, own0c, far0, far0c, own1, own1c, far1, far1c)
    blocks = [b.reshape(rows * nb, qa) for b in blocks]
    place = jnp.stack([lax.axis_index(a) for a in ("xh", "core", "z", "y")]).astype(jnp.int32)
    gathered = (w0, low0, high0) + opp0 + (w1, low1, high1) + opp1
    return contract(place, blocks, gathered, nk, qc).reshape(rows, nb, nk, qc)


def solution(mesh):
    fine = Mesh(mesh.devices.reshape(2, 2, 4, 4, 2), FINE)
    placed = P(None, ROW, None, ("xh", "core"))
    return jax.shard_map(
        on_device, mesh=fine, in_specs=(placed, placed), out_specs=placed, check_vma=False
    )
```

```python
import jax
import jax.numpy as jnp
from jax import lax
from jax.experimental import pallas as pl
from jax.experimental.pallas import tpu as pltpu
from jax.sharding import Mesh, PartitionSpec as P

FINE = ("xh", "core", "z", "y", "xl")
ROW = ("z", "y", "xl")
SWAP = [(0, 1), (1, 0)]
UP = [(n, (n + 1) % 4) for n in range(4)]
DOWN = [(n, (n - 1) % 4) for n in range(4)]
ACROSS = [(n, (n + 2) % 4) for n in range(4)]
TILE = 384
OFFSETS = (0, 3, 1, 2)
COSTS = (15, 0.2, 0.2, 7, 0.5)
ANY = pl.BlockSpec(memory_space=pl.ANY)
tie = lax.optimization_barrier


def planes(gathered):
    own, low, high, first, last = gathered
    for offset, ref in zip(OFFSETS, (own, low, high)):
        yield offset, [(n, ref, n) for n in range(4)]
    yield OFFSETS[3], [(n, (first, last)[n // 2], n % 2) for n in range(4)]


def contract_kernel(place, *refs):
    left, gathered, refs = (refs[:4], refs[4:6]), (refs[6:11], refs[11:16]), refs[17:]
    out, lhs, mat, total, staged, lsem, wsem, osem = refs
    nb, qa = left[0][0].shape[2:]
    width = total.shape[1]
    tiles = total.shape[0] // TILE
    per_tile = TILE // (2 * nb)
    core, z0, y0, xh = place[0], place[1], place[2], place[3]
    steps = [(i, half) for i in range(2) for half in range(2)]

    def start_matrix(s):
        i, half = steps[s]
        slot = s % 2
        for outer, inner in planes(gathered[i]):
            for n, ref, index in inner:
                if i == 0:
                    z, y = lax.rem(z0 + outer, 4), lax.rem(y0 + OFFSETS[n], 4)
                else:
                    z, y = lax.rem(z0 + OFFSETS[n], 4), lax.rem(y0 + outer, 4)

                @pl.when(z // 2 == half)
                def _(z=z, y=y, ref=ref, index=index):
                    pltpu.make_async_copy(
                        ref.at[index], mat.at[slot, lax.rem(z, 2), y], wsem.at[slot]
                    ).start()

    def start_left(s):
        i, half = steps[s]
        slot = s % 2
        for n, c in enumerate((core, 1 - core)):
            lanes = pl.ds(pl.multiple_of(c * qa, 128), qa)
            if i == 1:
                for xl in range(2):
                    pltpu.make_async_copy(
                        left[1][n].at[2 * half + xl], lhs.at[slot, :, xl, :, lanes], lsem.at[slot]
                    ).start()
                continue
            for ref, here in ((left[0][n], xh), (left[0][2 + n], 1 - xh)):

                @pl.when(here == half)
                def _(ref=ref, lanes=lanes):
                    pltpu.make_async_copy(ref, lhs.at[slot, :, :, :, lanes], lsem.at[slot]).start()

    def wait(buffer, sem, slot):
        pltpu.make_async_copy(buffer.at[slot], buffer.at[slot], sem.at[slot]).wait()

    start_matrix(0)
    start_left(0)
    stores = []
    for s in range(len(steps)):
        slot = s % 2
        if s + 1 < len(steps):
            start_matrix(s + 1)
            start_left(s + 1)
        wait(mat, wsem, slot)
        wait(lhs, lsem, slot)
        matrix = mat[slot].reshape(2 * qa, width)
        for m in range(tiles):
            at = pl.ds(m * TILE, TILE)
            rows = lhs[slot, m * per_tile : (m + 1) * per_tile].reshape(TILE, 2 * qa)
            term = jnp.dot(rows, matrix, preferred_element_type=jnp.float32)
            if s:
                term = term + total[at, :]
            if s + 1 < len(steps):
                total[at, :] = term
                continue
            staged[at] = term.astype(staged.dtype).reshape((TILE,) + staged.shape[1:])
            stores.append(pltpu.make_async_copy(staged.at[at], out.at[at], osem.at[m]))
            stores[-1].start()
    for c in stores:
        c.wait()


def contract(place, left, gathered, nk, after):
    n_zy = lax.axis_size(("z", "y"))
    nb, qa = left[0].shape[2:]
    rows, width = 2 * n_zy * nb, gathered[0].shape[2]
    dma = pltpu.SemaphoreType.DMA
    shape = jax.ShapeDtypeStruct((rows, nk, width // nk), jnp.bfloat16)
    return pl.pallas_call(
        contract_kernel,
        out_shape=shape,
        in_specs=[pl.BlockSpec(memory_space=pltpu.SMEM)] + [ANY] * 17,
        out_specs=ANY,
        scratch_shapes=[
            pltpu.VMEM((2, n_zy, 2, nb, 2 * qa), jnp.bfloat16),
            pltpu.VMEM((2, 2, 4) + gathered[0].shape[1:], jnp.bfloat16),
            pltpu.VMEM((rows, width), jnp.float32),
            pltpu.VMEM(shape.shape, shape.dtype),
            dma((2,)),
            dma((2,)),
            dma((rows // TILE,)),
        ],
        compiler_params=pltpu.CompilerParams(vmem_limit_bytes=40 << 20),
        cost_estimate=pl.CostEstimate(
            flops=2 * rows * 8 * qa * width, bytes_accessed=24 << 20, transcendentals=0
        ),
        name="contract",
    )(place, *left, *gathered, after)


def order(token, us, vmem=1):
    def body(t, o):
        o[...] = t[...]

    return pl.pallas_call(
        body,
        out_shape=jax.ShapeDtypeStruct(token.shape, token.dtype),
        compiler_params=pltpu.CompilerParams(vmem_limit_bytes=vmem << 20),
        cost_estimate=pl.CostEstimate(
            flops=int(us * 1.15e9), bytes_accessed=8192, transcendentals=0
        ),
        name="order",
    )(token)


def inner_ring(block, axis):
    moved = [lax.ppermute(block, axis, way) for way in (UP, DOWN, ACROSS)]
    return jnp.concatenate([block] + moved, axis=0)


def outer_ring(held, axis):
    return lax.ppermute(held, axis, UP), lax.ppermute(held, axis, DOWN)


def opposite(low, high, axis):
    return lax.ppermute(low[:2], axis, UP), lax.ppermute(high[2:], axis, DOWN)


def on_device(amplitudes, coupling):
    ni, _, v, qa = amplitudes.shape
    nb = v // lax.axis_size(ROW)
    n_zy = lax.axis_size(("z", "y"))
    na, nk, qc = coupling.shape[1:]
    token = jnp.zeros((8, 128), jnp.float32) + coupling[0, 0, 0, 0].astype(jnp.float32)

    def exchange(block, axes):
        return lax.all_to_all(block, axes, split_axis=0, concat_axis=0, tiled=True)

    def beside(block):
        return lax.ppermute(block, "core", SWAP)

    mine = coupling.reshape(ni, na, nk * qc)
    other = lax.ppermute(mine, "xl", SWAP)
    own0 = exchange(amplitudes[0, 0].reshape(n_zy * 2, nb, qa), ROW)
    part1 = amplitudes[1, 0].reshape(n_zy, 2, nb, qa)
    lower = lax.axis_index("xl") == 0
    pair = jnp.concatenate([jnp.where(lower, mine, other), jnp.where(lower, other, mine)], axis=1)

    w0 = inner_ring(pair[0][None], "y")
    w1 = inner_ring(pair[1][None], "z")
    token, own0, w0, w1, part1 = tie((token, own0, w0, w1, part1))

    zy1 = exchange(part1, ("z", "y"))
    token = order(token, COSTS[0])
    token, w0, w1, own0 = tie((token, w0, w1, own0))

    low0, high0 = outer_ring(w0, "z")
    low1, high1 = outer_ring(w1, "y")
    far0 = lax.ppermute(own0, "xh", SWAP)
    token = order(token, COSTS[1])
    token, zy1 = tie((token, zy1))
    zy1 = zy1.transpose(1, 0, 2, 3)
    x1 = exchange(jnp.concatenate([zy1, zy1], axis=0), ("xh", "xl"))
    token = order(token, COSTS[2])
    token, low0, high0, low1, high1, far0 = tie((token, low0, high0, low1, high1, far0))

    opp0 = opposite(low0, high0, "z")
    opp1 = opposite(low1, high1, "y")
    far0c = beside(far0)
    token = order(token, COSTS[3], 60)
    token, opp0, opp1, far0c, own0 = tie((token, opp0, opp1, far0c, own0))
    own0c = beside(own0)
    token = order(token, COSTS[4])
    token, x1 = tie((token, x1))
    x1c = beside(x1)

    place = jnp.stack([lax.axis_index(a) for a in ("core", "z", "y", "xh")]).astype(jnp.int32)
    left = tuple(b.reshape(n_zy, 2, nb, qa) for b in (own0, own0c, far0, far0c)) + (x1, x1c)
    gathered = (w0, low0, high0) + opp0 + (w1, low1, high1) + opp1
    return contract(place, left, gathered, nk, token).reshape(2 * n_zy, nb, nk, qc)


def solution(mesh):
    fine = Mesh(mesh.devices.reshape(2, 2, 4, 4, 2), FINE)
    placed = P(None, ROW, None, ("xh", "core"))
    return jax.shard_map(
        on_device, mesh=fine, in_specs=(placed, placed), out_specs=placed, check_vma=False
    )
```

```python
import functools

import jax
import jax.numpy as jnp
from jax import lax
from jax.experimental import pallas as pl
from jax.experimental.pallas import tpu as pltpu
from jax.sharding import Mesh, PartitionSpec as P

FINE = ("xh", "core", "z", "y", "xl")
ROW = ("z", "y", "xl")
SWAP = [(0, 1), (1, 0)]
UP = [(n, (n + 1) % 4) for n in range(4)]
DOWN = [(n, (n - 1) % 4) for n in range(4)]
ACROSS = [(n, (n + 2) % 4) for n in range(4)]
TILE = 384
OFFSETS = (0, 3, 1, 2)
COSTS = (15, 0.2, 0.2, 0.5, 0.2)
ANY = pl.BlockSpec(memory_space=pl.ANY)
tie = lax.optimization_barrier


def planes(gathered):
    own, low, high, first, last = gathered
    for offset, ref in zip(OFFSETS, (own, low, high)):
        yield offset, [(n, ref, n) for n in range(4)]
    yield OFFSETS[3], [(n, (first, last)[n // 2], n % 2) for n in range(4)]


def contract_kernel(last, place, *refs):
    left0, refs = refs[:4], refs[4:]
    if last:
        left1, across, gathered, so_far, refs = refs[:2], refs[2:4], refs[4:9], refs[9], refs[11:]
        out, lhs, mat, total, staged, lsem, wsem, tsem, osem = refs
        steps = (None, 0, 1)
    else:
        gathered, (out, lhs, mat, total, lsem, wsem, osem) = refs[:3], refs[3:]
        steps = (0, 1)
    nb, qa = left0[0].shape[2:]
    rows, width = total.shape
    tiles = rows // TILE
    per_tile = TILE // (2 * nb)
    core, z0, y0, xh = place[0], place[1], place[2], place[3]
    away = lax.rem(z0 + 2, 4)

    def copy_block(ref, index, slot, z, y):
        pltpu.make_async_copy(ref.at[index], mat.at[slot, z, y], wsem.at[slot, z]).start()

    def start_matrix(s):
        slot = s % 2
        if steps[s] is None:
            for n in range(4):
                copy_block(across[n // 2], n % 2, slot, 0, lax.rem(y0 + OFFSETS[n], 4))
            return
        blocks = (
            planes(gathered)
            if last
            else [(o, [(n, ref, n) for n in range(4)]) for o, ref in zip(OFFSETS, gathered)]
        )
        for outer, inner in blocks:
            for n, ref, index in inner:
                if last:
                    z, y = lax.rem(z0 + OFFSETS[n], 4), lax.rem(y0 + outer, 4)
                else:
                    z, y = lax.rem(z0 + outer, 4), lax.rem(y0 + OFFSETS[n], 4)

                @pl.when(z // 2 == steps[s])
                def _(z=z, y=y, ref=ref, index=index):
                    copy_block(ref, index, slot, lax.rem(z, 2), y)

    def wait_matrix(s):
        slot = s % 2
        for z in range(1 if steps[s] is None else 2):
            part = mat.at[slot, z]
            if last:
                pltpu.make_async_copy(part, part, wsem.at[slot, z]).wait()
                continue
            absent = away == 2 * steps[s] + z

            @pl.when(jnp.logical_not(absent))
            def _(part=part, z=z):
                pltpu.make_async_copy(part, part, wsem.at[slot, z]).wait()

            @pl.when(absent)
            def _(part=part):
                part[...] = jnp.zeros(part.shape, part.dtype)

    def left_part(s):
        return lhs.at[s % 2, :, :, :, :qa] if steps[s] is None else lhs.at[s % 2]

    def start_left(s):
        slot, half = s % 2, steps[s]
        for n, c in enumerate((core, 1 - core)):
            lanes = pl.ds(pl.multiple_of(c * qa, 128), qa)
            if last and half is not None:
                for xl in range(2):
                    pltpu.make_async_copy(
                        left1[n].at[2 * half + xl], lhs.at[slot, :, xl, :, lanes], lsem.at[slot]
                    ).start()
                continue
            for ref, here in ((left0[n], xh), (left0[2 + n], 1 - xh)):
                if half is None:
                    wanted, target = away == 2 * here + c, left_part(s)
                else:
                    wanted, target = here == half, lhs.at[slot, :, :, :, lanes]

                @pl.when(wanted)
                def _(ref=ref, target=target):
                    pltpu.make_async_copy(ref, target, lsem.at[slot]).start()

    def at(m):
        return pl.ds(m * TILE, TILE)

    start_matrix(0)
    start_left(0)
    sums = []
    if last:
        for m in range(tiles):
            sums.append(pltpu.make_async_copy(so_far.at[at(m)], total.at[at(m)], tsem.at[m]))
            sums[-1].start()
    stores = []
    for s in range(len(steps)):
        slot = s % 2
        if s + 1 < len(steps):
            start_matrix(s + 1)
            start_left(s + 1)
        wait_matrix(s)
        pltpu.make_async_copy(left_part(s), left_part(s), lsem.at[slot]).wait()
        depth = qa if steps[s] is None else 2 * qa
        if steps[s] is None:
            matrix = mat[slot, 0].reshape(depth, width)
        else:
            matrix = mat[slot].reshape(depth, width)
        for m in range(tiles):
            some = lhs[slot, m * per_tile : (m + 1) * per_tile, :, :, :depth].reshape(TILE, depth)
            term = jnp.dot(some, matrix, preferred_element_type=jnp.float32)
            if last and s == 0:
                sums[m].wait()
            if last or s:
                term = term + total[at(m), :]
            end = s + 1 == len(steps)
            if last and end:
                staged[at(m)] = term.astype(staged.dtype).reshape((TILE,) + staged.shape[1:])
            else:
                total[at(m), :] = term
            if end:
                source = staged if last else total
                stores.append(pltpu.make_async_copy(source.at[at(m)], out.at[at(m)], osem.at[m]))
                stores[-1].start()
    for c in stores:
        c.wait()


def contract(place, operands, shape, cost):
    last = shape.dtype == jnp.bfloat16
    n_zy = lax.axis_size(("z", "y"))
    nb, qa = operands[0].shape[2:]
    block = operands[4 if not last else 8].shape[1:]
    rows = 2 * n_zy * nb
    dma = pltpu.SemaphoreType.DMA
    scratch = [
        pltpu.VMEM((2, n_zy, 2, nb, 2 * qa), jnp.bfloat16),
        pltpu.VMEM((2, 2, 4) + block, jnp.bfloat16),
        pltpu.VMEM((rows, block[1]), jnp.float32),
    ]
    sems = [dma((2,)), dma((2, 2)), dma((rows // TILE,))]
    if last:
        scratch.append(pltpu.VMEM(shape.shape, shape.dtype))
        sems.append(dma((rows // TILE,)))
    return pl.pallas_call(
        functools.partial(contract_kernel, last),
        out_shape=shape,
        in_specs=[pl.BlockSpec(memory_space=pltpu.SMEM)] + [ANY] * len(operands),
        out_specs=ANY,
        scratch_shapes=scratch + sems,
        compiler_params=pltpu.CompilerParams(vmem_limit_bytes=40 << 20),
        cost_estimate=pl.CostEstimate(
            flops=int(cost * 1.15e9), bytes_accessed=1 << 20, transcendentals=0
        ),
        name="contract_last" if last else "contract_first",
    )(place, *operands)


def order(token, us, vmem=1):
    def body(t, o):
        o[...] = t[...]

    return pl.pallas_call(
        body,
        out_shape=jax.ShapeDtypeStruct(token.shape, token.dtype),
        compiler_params=pltpu.CompilerParams(vmem_limit_bytes=vmem << 20),
        cost_estimate=pl.CostEstimate(
            flops=int(us * 1.15e9), bytes_accessed=8192, transcendentals=0
        ),
        name="order",
    )(token)


def inner_ring(block, axis):
    moved = [lax.ppermute(block, axis, way) for way in (UP, DOWN, ACROSS)]
    return jnp.concatenate([block] + moved, axis=0)


def outer_ring(held, axis):
    return lax.ppermute(held, axis, UP), lax.ppermute(held, axis, DOWN)


def opposite(low, high, axis):
    return lax.ppermute(low[:2], axis, UP), lax.ppermute(high[2:], axis, DOWN)


def on_device(amplitudes, coupling):
    ni, _, v, qa = amplitudes.shape
    nb = v // lax.axis_size(ROW)
    n_zy = lax.axis_size(("z", "y"))
    na, nk, qc = coupling.shape[1:]
    token = jnp.zeros((8, 128), jnp.float32) + coupling[0, 0, 0, 0].astype(jnp.float32)

    def exchange(block, axes):
        return lax.all_to_all(block, axes, split_axis=0, concat_axis=0, tiled=True)

    def beside(block):
        return lax.ppermute(block, "core", SWAP)

    mine = coupling.reshape(ni, na, nk * qc)
    other = lax.ppermute(mine, "xl", SWAP)
    own0 = exchange(amplitudes[0, 0].reshape(n_zy * 2, nb, qa), ROW)
    part1 = amplitudes[1, 0].reshape(n_zy, 2, nb, qa)
    lower = lax.axis_index("xl") == 0
    pair = jnp.concatenate([jnp.where(lower, mine, other), jnp.where(lower, other, mine)], axis=1)

    w0 = inner_ring(pair[0][None], "y")
    w1 = inner_ring(pair[1][None], "z")
    token, own0, w0, w1, part1 = tie((token, own0, w0, w1, part1))

    zy1 = exchange(part1, ("z", "y"))
    token = order(token, COSTS[0])
    token, w0, w1, own0 = tie((token, w0, w1, own0))

    low0, high0 = outer_ring(w0, "z")
    low1, high1 = outer_ring(w1, "y")
    far0 = lax.ppermute(own0, "xh", SWAP)
    token = order(token, COSTS[1])
    token, zy1 = tie((token, zy1))
    zy1 = zy1.transpose(1, 0, 2, 3)
    x1 = exchange(jnp.concatenate([zy1, zy1], axis=0), ("xh", "xl"))
    token = order(token, COSTS[2])
    token, low0, high0, low1, high1, far0 = tie((token, low0, high0, low1, high1, far0))

    opp0 = opposite(low0, high0, "z")
    opp1 = opposite(low1, high1, "y")
    far0c, own0c = beside(far0), beside(own0)
    place = jnp.stack([lax.axis_index(a) for a in ("core", "z", "y", "xh")]).astype(jnp.int32)
    left0 = tuple(b.reshape(n_zy, 2, nb, qa) for b in (own0, own0c, far0, far0c))
    rows = 2 * n_zy * nb
    total = jax.ShapeDtypeStruct((rows, nk * qc), jnp.float32)
    total = contract(place, left0 + (w0, low0, high0), total, COSTS[3])
    token, total, opp0, opp1 = tie((token, total, opp0, opp1))
    token = order(token, COSTS[4], 60)
    token, x1 = tie((token, x1))

    operands = left0 + (x1, beside(x1)) + opp0 + (w1, low1, high1) + opp1 + (total, token)
    result = jax.ShapeDtypeStruct((rows, nk, qc), jnp.bfloat16)
    return contract(place, operands, result, 12).reshape(2 * n_zy, nb, nk, qc)


def solution(mesh):
    fine = Mesh(mesh.devices.reshape(2, 2, 4, 4, 2), FINE)
    placed = P(None, ROW, None, ("xh", "core"))
    return jax.shard_map(
        on_device, mesh=fine, in_specs=(placed, placed), out_specs=placed, check_vma=False
    )
```
